256 devices in a mesh: kv: 8 (over x, y_hi), ctx: 32 (over z, y_lo, core).
Axes of the slice: x: 4, y: 4 (y_hi: 2, y_lo: 2; y = y_hi * 2 + y_lo), z: 8, core: 2. Of those that a mesh axis runs over, the one named last changes fastest.
Arguments:
- queries: bfloat16 [2, 64, 16384], P(None, 'kv'), may hold values from -105 to 105
- kv_cache: bfloat16 [8, 4, 131072, 256], P('kv', None, 'ctx'), may hold values from -5 to 5
- lengths: int32 [64], replicated, may hold values from 16384 to 131071, as said below
Outputs:
- attended: bfloat16 [2, 64, 16384], P(None, 'ctx', 'kv')
The draws below stay inside these ranges and needn't reach their ends.
Inputs may be any that keep to these rules, and one draw needn't show every extreme that they name: Row r reads lengths[r] + t positions at step t; some row reads exactly 16384 and some row reaches the most.
All inputs are finite; a program needn't handle non-finite values.
Results may differ from the reference program's by a relative error of at most 0.0048.
Values may be sent and summed in bfloat16 or wider, within the bound.
A program may use at most 192 MiB of HBM per device.

```python
import jax
import jax.numpy as jnp
from jax import lax

QUERY_HEADS = 128
KEY_VALUE_HEADS = 8
HEAD_SIZE = 128
STEPS = 2
ROLLOUT_COUNT = 16
PROMPT_COUNT = 4
CTX_DEV = 4096
ROWS = 64
PROMPT_POSITIONS = 131072
N_CTX = 32


def key_field(key):
    return jnp.clip(jax.random.normal(jax.random.fold_in(key, 77), (KEY_VALUE_HEADS, PROMPT_COUNT, PROMPT_POSITIONS, HEAD_SIZE), jnp.float32), -5.0, 5.0)


def draw_kv_cache(key, part):
    cached_keys = key_field(key)
    key = jax.random.fold_in(key, 1)
    cached_values = jnp.clip(jax.random.normal(jax.random.fold_in(key, 3), (KEY_VALUE_HEADS, PROMPT_COUNT, PROMPT_POSITIONS, HEAD_SIZE), jnp.float32), -5.0, 5.0)
    return jnp.concatenate([cached_keys, cached_values], axis=-1).astype(jnp.bfloat16)


def draw_queries(key, part):
    key = jax.random.fold_in(key, 2)
    drawn = jnp.clip(jax.random.normal(key, (STEPS, ROWS, QUERY_HEADS, HEAD_SIZE), jnp.float32), -5.0, 5.0)
    return drawn.reshape(STEPS, ROWS, QUERY_HEADS * HEAD_SIZE).astype(jnp.bfloat16)


def draw_lengths(key, part):
    key = jax.random.fold_in(key, 5)
    longest = PROMPT_POSITIONS - STEPS + 1
    shortest = PROMPT_POSITIONS // 8
    drawn = jax.random.randint(jax.random.fold_in(key, 1), (ROWS,), shortest, longest + 1)
    high_row = jax.random.randint(jax.random.fold_in(key, 2), (), 0, ROWS)
    low_row = (high_row + ROWS // 2) % ROWS
    drawn = drawn.at[high_row].set(longest)
    drawn = drawn.at[low_row].set(shortest)
    return drawn.astype(jnp.int32)


def setup_inputs(seed: int = 0) -> dict:
    key_of = jax.random.split(jax.random.key(seed), 4)
    queries = draw_queries(jax.random.fold_in(key_of[3], 71), 0)
    kv_cache = draw_kv_cache(jax.random.fold_in(key_of[3], 71), 0)
    lengths = draw_lengths(jax.random.fold_in(key_of[3], 71), 0)
    return {"queries": queries, "kv_cache": kv_cache, "lengths": lengths}


MASK_FILLER = -1e30


def shard_terms(rollout_queries, cached_keys, cached_values, limits, offset, span_width):
    scores = jnp.einsum("srkgd,kscd->srkgc", rollout_queries.astype(jnp.float32), cached_keys.astype(jnp.float32)) * (rollout_queries.shape[-1] ** -0.5)
    positions = offset + jnp.arange(span_width, dtype=jnp.int32)
    visible = positions[None, None, None, None, :] < limits[:, :, None, None, None]
    masked = jnp.where(visible, scores, MASK_FILLER)
    row_max = jnp.max(masked, axis=-1)
    weights = jnp.where(visible, jnp.exp(masked - row_max[..., None]), 0.0)
    row_sum = jnp.sum(weights, axis=-1)
    rounded = lax.optimization_barrier(weights.astype(jnp.bfloat16)).astype(jnp.float32)
    weighted = jnp.einsum("srkgc,kscd->srkgd", rounded, cached_values.astype(jnp.float32))
    return row_max, row_sum, weighted


def combine(first, second):
    highest = jnp.maximum(first[0], second[0])
    first_factor = jnp.exp(first[0] - highest)
    second_factor = jnp.exp(second[0] - highest)
    total = first[1] * first_factor + second[1] * second_factor
    weighted = first[2] * first_factor[..., None] + second[2] * second_factor[..., None]
    return highest, total, weighted


def reference(queries, kv_cache, lengths):
    queries_per_group = QUERY_HEADS // KEY_VALUE_HEADS
    outputs = []
    for decode_step_index in range(STEPS):
        rollout_queries = queries[decode_step_index].reshape(PROMPT_COUNT, ROLLOUT_COUNT, KEY_VALUE_HEADS, queries_per_group, HEAD_SIZE)
        limits = (lengths + decode_step_index).reshape(PROMPT_COUNT, ROLLOUT_COUNT)

        def visit_shard(carried, shard_index):
            cache_block = lax.dynamic_slice_in_dim(kv_cache, shard_index * CTX_DEV, CTX_DEV, 2)
            partials = shard_terms(rollout_queries, cache_block[..., :HEAD_SIZE], cache_block[..., HEAD_SIZE:], limits, shard_index * CTX_DEV, CTX_DEV)
            return combine(carried, partials), None

        starting_state = (jnp.full((PROMPT_COUNT, ROLLOUT_COUNT, KEY_VALUE_HEADS, queries_per_group), MASK_FILLER, jnp.float32),
                   jnp.zeros((PROMPT_COUNT, ROLLOUT_COUNT, KEY_VALUE_HEADS, queries_per_group), jnp.float32),
                   jnp.zeros((PROMPT_COUNT, ROLLOUT_COUNT, KEY_VALUE_HEADS, queries_per_group, HEAD_SIZE), jnp.float32))
        finished, _ = lax.scan(visit_shard, starting_state, jnp.arange(N_CTX, dtype=jnp.int32))
        result = finished[2] / finished[1][..., None]
        outputs.append(result.reshape(ROWS, QUERY_HEADS * HEAD_SIZE).astype(jnp.bfloat16))
    return jnp.stack(outputs)
```

```python
import functools

import jax
import jax.numpy as jnp
from jax import lax
from jax.experimental import pallas as pl
from jax.experimental.pallas import tpu as pltpu
from jax.sharding import PartitionSpec as P

F32, BF16 = jnp.float32, jnp.bfloat16
STEPS, ROWS, GROUP, HEAD = 2, 64, 16, 128
UNITS, PROMPTS, SPAN = 8, 4, 4096
UNIT_ROWS = STEPS * (ROWS // UNITS) * GROUP
SCALE = 1.4426950408889634 / HEAD**0.5
HIDE = 2.0**20
CHUNK = 1024


def nt(a, b):
    return lax.dot_general(a, b, (((1,), (1,)), ((), ())), preferred_element_type=F32)


def limit_lanes(lengths_ref):
    lane = lax.broadcasted_iota(jnp.int32, (8, 128), 1)
    row = lane % ROWS
    held = jnp.zeros((8, 128), jnp.int32)
    for r in range(ROWS):
        held = jnp.where(row == r, lengths_ref[r], held)
    return held + lane // ROWS


def attend(lengths_ref, q_ref, kv_hbm, o_ref, lse_ref, kv, hide, s0, s1, sems):
    scores = (s0, s1)
    for p in range(PROMPTS):
        pltpu.make_async_copy(kv_hbm.at[0, p], kv.at[p], sems.at[p]).start()
    limits = limit_lanes(lengths_ref) - lax.axis_index("ctx") * SPAN

    def fill(i, _):
        position = lax.broadcasted_iota(jnp.int32, (64, 128), 0) + i * 64
        at = pl.ds(pl.multiple_of(i * 64, 64), 64)
        hide[at, :] = jnp.where(position < limits[0:1, :], 0.0, -HIDE).astype(BF16)
        return 0

    lax.fori_loop(0, SPAN // 64, fill, 0)

    def wait(p):
        pltpu.make_async_copy(kv_hbm.at[0, p], kv.at[p], sems.at[p]).wait()

    def marked(u):
        i = lax.broadcasted_iota(jnp.int32, (UNIT_ROWS, 128), 0)
        lane = lax.broadcasted_iota(jnp.int32, (UNIT_ROWS, 128), 1)
        target = (i // 128) * ROWS + u * 8 + (i % 128) // GROUP
        return jnp.concatenate([q_ref[u], (lane == target).astype(BF16)], axis=1)

    ones = jnp.ones((CHUNK, 128), BF16)

    def stage(u, n, use, make, top):
        if u is not None:
            peak = jnp.max(top, axis=1, keepdims=True) * SCALE
            total = None
        if n is not None:
            q = marked(n)
            new_top = None
        for c in range(SPAN // CHUNK):
            at = slice(c * CHUNK, (c + 1) * CHUNK)
            if n is not None:
                k = jnp.concatenate([kv[n // 2, at, 0:HEAD], hide[at, :]], axis=1)
                s = nt(q, k)
                scores[make][:, at] = s
                for b in range(CHUNK // 128):
                    x = s[:, b * 128 : (b + 1) * 128]
                    new_top = x if new_top is None else jnp.maximum(new_top, x)
            if u is not None:
                w = jnp.exp2(scores[use][:, at] * SCALE - peak).astype(BF16)
                v = jnp.concatenate([kv[u // 2, at, HEAD : 2 * HEAD], ones], axis=1)
                part = jnp.dot(w, v, preferred_element_type=F32)
                total = part if total is None else total + part
        if u is not None:
            weight = total[:, HEAD:]
            o = (total[:, :HEAD] / weight).astype(BF16)
            lse = jnp.log2(weight) + peak
            for d in range(4):
                for t in range(STEPS):
                    src = slice(t * 128 + d * 32, t * 128 + d * 32 + 32)
                    o_ref[4 * u + d, t * 32 : t * 32 + 32, :] = o[src, :]
                    lse_ref[4 * u + d, t * 32 : t * 32 + 32, :] = lse[src, :]
        return new_top if n is not None else None

    wait(0)
    top = stage(None, 0, 1, 0, None)

    def pair(i, top):
        u = i * 2
        top = stage(u, u + 1, 0, 1, top)
        wait(i + 1)
        return stage(u + 1, u + 2, 1, 0, top)

    top = lax.fori_loop(0, UNITS // 2 - 1, pair, top)
    top = stage(UNITS - 2, UNITS - 1, 0, 1, top)
    stage(UNITS - 1, None, 1, None, top)


def shards(queries, kv_cache, lengths):
    sent = queries.reshape(STEPS, 8, 8, GROUP, HEAD).transpose(2, 0, 1, 3, 4)
    held = lax.all_to_all(sent, "kv", split_axis=0, concat_axis=0)
    held = held.reshape(UNITS, UNIT_ROWS, HEAD)
    o, lse = pl.pallas_call(
        attend,
        out_shape=[
            jax.ShapeDtypeStruct((32, 64, HEAD), BF16),
            jax.ShapeDtypeStruct((32, 64, HEAD), F32),
        ],
        in_specs=[
            pl.BlockSpec(memory_space=pltpu.SMEM),
            pl.BlockSpec(memory_space=pltpu.VMEM),
            pl.BlockSpec(memory_space=pl.ANY),
        ],
        out_specs=[pl.BlockSpec(memory_space=pltpu.VMEM)] * 2,
        scratch_shapes=[
            pltpu.VMEM((PROMPTS, SPAN, 2 * HEAD), BF16),
            pltpu.VMEM((SPAN, 128), BF16),
            pltpu.VMEM((UNIT_ROWS, SPAN), F32),
            pltpu.VMEM((UNIT_ROWS, SPAN), F32),
            pltpu.SemaphoreType.DMA((PROMPTS,)),
        ],
        compiler_params=pltpu.CompilerParams(vmem_limit_bytes=50 * 2**20),
        name="attend",
    )(lengths, held, kv_cache)
    o = lax.all_to_all(o, "ctx", split_axis=0, concat_axis=0)
    lse = lax.all_to_all(lse[:, :, 0], "ctx", split_axis=0, concat_axis=0)
    factor = jnp.exp2(lse - jnp.max(lse, axis=0, keepdims=True))
    total = jnp.sum(factor, axis=0)[:, None]
    out = jnp.sum(o.astype(F32) * factor[:, :, None], axis=0) / total
    return out.astype(BF16).reshape(STEPS, 2, GROUP * HEAD)


def solution(mesh):
    in_specs = (P(None, "kv", None), P("kv", None, "ctx", None), P())
    out_specs = P(None, "ctx", "kv")
    return jax.shard_map(shards, mesh=mesh, in_specs=in_specs, out_specs=out_specs, check_vma=False)
```

```python
import jax
import jax.numpy as jnp
from jax import lax
from jax.experimental import pallas as pl
from jax.experimental.pallas import tpu as pltpu
from jax.sharding import PartitionSpec as P

F32, BF16 = jnp.float32, jnp.bfloat16
STEPS, ROWS, GROUP, HEAD = 2, 64, 16, 128
UNITS, PROMPTS, SPAN = 8, 4, 4096
UNIT_ROWS = STEPS * (ROWS // UNITS) * GROUP
PART = UNIT_ROWS // 4
BLOCK = PART + 16
SCALE = 1.4426950408889634 / HEAD**0.5
HIDE = 2.0**20
CHUNK = 1024
MESH = pl.DeviceIdType.MESH


def nt(a, b):
    return lax.dot_general(a, b, (((1,), (1,)), ((), ())), preferred_element_type=F32)


def limit_lanes(lengths_ref):
    lane = lax.broadcasted_iota(jnp.int32, (8, 128), 1)
    row = lane % ROWS
    held = jnp.zeros((8, 128), jnp.int32)
    for r in range(ROWS):
        held = jnp.where(row == r, lengths_ref[r], held)
    return held + lane // ROWS


def pack(lse, base):
    rows = lse[0].shape[0]
    sub = lax.broadcasted_iota(jnp.int32, (rows, 128), 0)
    lane = lax.broadcasted_iota(jnp.int32, (rows, 128), 1)
    at = lax.broadcasted_iota(jnp.int32, (16, 128), 0)
    tile = jnp.zeros((16, 128), F32)
    for t in range(STEPS):
        x = jnp.sum(jnp.where(lane == sub + base, lse[t], 0.0), axis=0, keepdims=True)
        high = x.astype(BF16).astype(F32)
        rest = x - high
        middle = rest.astype(BF16).astype(F32)
        for k, term in enumerate((high, middle, rest - middle)):
            tile = jnp.where(at == 2 * k + t, term, tile)
    return tile.astype(BF16)


def unpack(block, base):
    o = block[0:PART].astype(F32)
    tile = block[PART:BLOCK].astype(F32)
    half = PART // STEPS
    sub = lax.broadcasted_iota(jnp.int32, (half, 128), 0)
    lane = lax.broadcasted_iota(jnp.int32, (half, 128), 1)
    lse = []
    for t in range(STEPS):
        x = tile[t : t + 1] + tile[2 + t : 3 + t] + tile[4 + t : 5 + t]
        spread = jnp.where(lane == sub + base, jnp.broadcast_to(x, (half, 128)), 0.0)
        lse.append(jnp.sum(spread, axis=1, keepdims=True))
    return o, jnp.concatenate(lse, axis=0)


def merge(parts):
    top = parts[0][1]
    for _, lse in parts[1:]:
        top = jnp.maximum(top, lse)
    total, weighted = None, None
    for o, lse in parts:
        factor = jnp.exp2(lse - top)
        total = factor if total is None else total + factor
        weighted = o * factor if weighted is None else weighted + o * factor
    return weighted / total, jnp.log2(total) + top


def attend(
    lengths_ref, q_hbm, kv_hbm, out_ref,
    kv, qs, hide, s0, s1, psend, precv, zsend, zrecv,
    kv_sem, own_sem, q_out, q_in, p_out, p_in, z_out, z_in,
):
    scores = (s0, s1)
    me = lax.axis_index("kv")
    ctx = lax.axis_index("ctx")
    plane = ctx // 4
    place = ctx % 4
    flip = 2 - 4 * (place // 2)
    last = (plane - me + UNITS) % UNITS
    base = place * (PART // STEPS)

    def unit_at(i):
        after = jnp.where(i >= last, i + 1, i)
        return (me + after) % UNITS

    def wait_kv(p):
        pltpu.make_async_copy(kv_hbm.at[0, p], kv.at[p], kv_sem.at[p]).wait()

    def query_copy(k, source):
        across = (k + me) % 2
        return pltpu.make_async_remote_copy(
            src_ref=q_hbm.at[k],
            dst_ref=qs.at[source],
            send_sem=q_out.at[k],
            recv_sem=q_in.at[source],
            device_id=(k, ctx + across * flip),
            device_id_type=MESH,
        )

    def plane_copy(i, o):
        there = (place + o) % 4
        return pltpu.make_async_remote_copy(
            src_ref=psend.at[i, there],
            dst_ref=precv.at[i, o - 1],
            send_sem=p_out.at[i, o - 1],
            recv_sem=p_in.at[i, o - 1],
            device_id=(me, plane * 4 + there),
            device_id_type=MESH,
        )

    def z_copy(i, z):
        return pltpu.make_async_remote_copy(
            src_ref=zsend.at[i],
            dst_ref=zrecv.at[plane],
            send_sem=z_out.at[i],
            recv_sem=z_in.at[plane],
            device_id=(me, z * 4 + place),
            device_id_type=MESH,
        )

    first = unit_at(0)
    for n in range(PROMPTS):
        p = (first // 2 + n) % PROMPTS
        pltpu.make_async_copy(kv_hbm.at[0, p], kv.at[p], kv_sem.at[p]).start()
    own = pltpu.make_async_copy(q_hbm.at[me], qs.at[me], own_sem)
    own.start()

    barrier = pltpu.get_barrier_semaphore()
    for n in range(1, UNITS):
        k = (me + n) % UNITS
        across = (k + me) % 2
        pl.semaphore_signal(barrier, inc=1, device_id=(k, ctx + across * flip), device_id_type=MESH)
        z = (plane + n) % UNITS
        pl.semaphore_signal(barrier, inc=1, device_id=(me, z * 4 + place), device_id_type=MESH)
    for o in range(1, 4):
        there = plane * 4 + (place + o) % 4
        pl.semaphore_signal(barrier, inc=1, device_id=(me, there), device_id_type=MESH)

    limits = limit_lanes(lengths_ref) - ctx * SPAN

    def fill(i, _):
        position = lax.broadcasted_iota(jnp.int32, (64, 128), 0) + i * 64
        at = pl.ds(pl.multiple_of(i * 64, 64), 64)
        hide[at, :] = jnp.where(position < limits[0:1, :], 0.0, -HIDE).astype(BF16)
        return 0

    lax.fori_loop(0, SPAN // 64, fill, 0)

    pl.semaphore_wait(barrier, 2 * (UNITS - 1) + 3)
    for n in range(1, UNITS):
        query_copy((me - n + UNITS) % UNITS, me).start()
    own.wait()

    def ready(i, u):
        @pl.when(u != me)
        def _():
            query_copy(u, u).wait_recv()

        mate = (u + 1 - 2 * (u % 2) - me + UNITS) % UNITS
        mate_at = jnp.where(mate == last, UNITS - 1, jnp.where(mate > last, mate - 1, mate))

        @pl.when(mate_at > i)
        def _():
            wait_kv(u // 2)

    def marked(u):
        i = lax.broadcasted_iota(jnp.int32, (UNIT_ROWS, 128), 0)
        lane = lax.broadcasted_iota(jnp.int32, (UNIT_ROWS, 128), 1)
        target = (i // 128) * ROWS + u * 8 + (i % 128) // GROUP
        return jnp.concatenate([qs[u], (lane == target).astype(BF16)], axis=1)

    ones = jnp.ones((CHUNK, 128), BF16)

    def stage(i, u, n, use, make, top):
        if u is not None:
            peak = jnp.max(top, axis=1, keepdims=True) * SCALE
            total = None
        if n is not None:
            q = marked(n)
            new_top = None
        for c in range(SPAN // CHUNK):
            at = slice(c * CHUNK, (c + 1) * CHUNK)
            if n is not None:
                k = jnp.concatenate([kv[n // 2, at, 0:HEAD], hide[at, :]], axis=1)
                s = nt(q, k)
                scores[make][:, at] = s
                for b in range(CHUNK // 128):
                    x = s[:, b * 128 : (b + 1) * 128]
                    new_top = x if new_top is None else jnp.maximum(new_top, x)
            if u is not None:
                w = jnp.exp2(scores[use][:, at] * SCALE - peak).astype(BF16)
                v = jnp.concatenate([kv[u // 2, at, HEAD : 2 * HEAD], ones], axis=1)
                part = jnp.dot(w, v, preferred_element_type=F32)
                total = part if total is None else total + part
        if u is not None:
            weight = total[:, HEAD:]
            o = (total[:, :HEAD] / weight).astype(BF16)
            lse = jnp.log2(weight) + peak
            sums = pack((lse[:128], lse[128:]), 0)
            for d in range(4):
                psend[i, d, 0:32, :] = o[d * 32 : d * 32 + 32]
                psend[i, d, 32:64, :] = o[128 + d * 32 : 160 + d * 32]
                psend[i, d, PART:BLOCK, :] = sums
        return new_top if n is not None else None

    def send_plane(i):
        for o in range(1, 4):
            plane_copy(i, o).start()

    def gather_plane(i):
        parts = [unpack(psend[i, place], base)]
        for o in range(1, 4):
            plane_copy(i, o).wait_recv()
            parts.append(unpack(precv[i, o - 1], base))
        return merge(parts)

    def pass_on(i):
        o, lse = gather_plane(i)
        half = PART // STEPS
        zsend[i, 0:PART, :] = o.astype(BF16)
        zsend[i, PART:BLOCK, :] = pack((lse[:half], lse[half:]), base)
        z_copy(i, unit_at(i)).start()

    ready(0, first)
    top = stage(0, None, first, 1, 0, None)

    def pair(h, top):
        i = 2 * h
        a, b, c = unit_at(i), unit_at(i + 1), unit_at(i + 2)
        ready(i + 1, b)
        top = stage(i, a, b, 0, 1, top)
        send_plane(i)

        @pl.when(h > 0)
        def _():
            pass_on(i - 1)

        ready(i + 2, c)
        top = stage(i + 1, b, c, 1, 0, top)
        send_plane(i + 1)
        pass_on(i)
        return top

    top = lax.fori_loop(0, UNITS // 2 - 1, pair, top)
    ready(UNITS - 1, plane)
    top = stage(UNITS - 2, unit_at(UNITS - 2), plane, 0, 1, top)
    send_plane(UNITS - 2)
    pass_on(UNITS - 3)
    stage(UNITS - 1, plane, None, 1, None, top)
    send_plane(UNITS - 1)
    pass_on(UNITS - 2)
    parts = [gather_plane(UNITS - 1)]
    for n in range(1, UNITS):
        z = (plane + n) % UNITS
        pltpu.make_async_remote_copy(
            src_ref=zsend.at[0],
            dst_ref=zrecv.at[z],
            send_sem=z_out.at[0],
            recv_sem=z_in.at[z],
            device_id=(me, z * 4 + place),
            device_id_type=MESH,
        ).wait_recv()
        parts.append(unpack(zrecv[z], base))
    out_ref[...] = merge(parts)[0].astype(BF16)

    for n in range(1, UNITS):
        query_copy((me - n + UNITS) % UNITS, me).wait_send()

    def sent(i, _):
        for o in range(1, 4):
            plane_copy(i, o).wait_send()
        return 0

    lax.fori_loop(0, UNITS, sent, 0)

    def sent_z(i, _):
        z_copy(i, unit_at(i)).wait_send()
        return 0

    lax.fori_loop(0, UNITS - 1, sent_z, 0)


def shards(queries, kv_cache, lengths):
    sent = queries.reshape(STEPS, 8, 8, GROUP, HEAD).transpose(2, 0, 1, 3, 4)
    out = pl.pallas_call(
        attend,
        out_shape=jax.ShapeDtypeStruct((PART, HEAD), BF16),
        in_specs=[
            pl.BlockSpec(memory_space=pltpu.SMEM),
            pl.BlockSpec(memory_space=pl.ANY),
            pl.BlockSpec(memory_space=pl.ANY),
        ],
        out_specs=pl.BlockSpec(memory_space=pltpu.VMEM),
        scratch_shapes=[
            pltpu.VMEM((PROMPTS, SPAN, 2 * HEAD), BF16),
            pltpu.VMEM((UNITS, UNIT_ROWS, HEAD), BF16),
            pltpu.VMEM((SPAN, 128), BF16),
            pltpu.VMEM((UNIT_ROWS, SPAN), F32),
            pltpu.VMEM((UNIT_ROWS, SPAN), F32),
            pltpu.VMEM((UNITS, 4, BLOCK, HEAD), BF16),
            pltpu.VMEM((UNITS, 3, BLOCK, HEAD), BF16),
            pltpu.VMEM((UNITS, BLOCK, HEAD), BF16),
            pltpu.VMEM((UNITS, BLOCK, HEAD), BF16),
            pltpu.SemaphoreType.DMA((PROMPTS,)),
            pltpu.SemaphoreType.DMA,
            pltpu.SemaphoreType.DMA((UNITS,)),
            pltpu.SemaphoreType.DMA((UNITS,)),
            pltpu.SemaphoreType.DMA((UNITS, 3)),
            pltpu.SemaphoreType.DMA((UNITS, 3)),
            pltpu.SemaphoreType.DMA((UNITS,)),
            pltpu.SemaphoreType.DMA((UNITS,)),
        ],
        compiler_params=pltpu.CompilerParams(
            vmem_limit_bytes=50 * 2**20, collective_id=0, has_side_effects=True
        ),
        name="attend",
    )(lengths, sent.reshape(UNITS, UNIT_ROWS, HEAD), kv_cache)
    return out.reshape(STEPS, 2, GROUP * HEAD)


def solution(mesh):
    in_specs = (P(None, "kv", None), P("kv", None, "ctx", None), P())
    out_specs = P(None, "ctx", "kv")
    return jax.shard_map(shards, mesh=mesh, in_specs=in_specs, out_specs=out_specs, check_vma=False)
```

```python
import jax
import jax.numpy as jnp
from jax import lax
from jax.experimental import pallas as pl
from jax.experimental.pallas import tpu as pltpu
from jax.sharding import PartitionSpec as P

F32, BF16 = jnp.float32, jnp.bfloat16
STEPS, ROWS, GROUP, HEAD = 2, 64, 16, 128
UNITS, PROMPTS, SPAN = 8, 4, 4096
WIDE = GROUP * HEAD
UNIT_ROWS = STEPS * GROUP * (ROWS // UNITS)
PART = UNIT_ROWS // 4
BLOCK = PART + 16
SCALE = 1.4426950408889634 / HEAD**0.5
HIDE = 2.0**20
CHUNK = 1024
MESH = pl.DeviceIdType.MESH


def nt(a, b):
    return lax.dot_general(a, b, (((1,), (1,)), ((), ())), preferred_element_type=F32)


def limit_lanes(lengths_ref):
    lane = lax.broadcasted_iota(jnp.int32, (8, 128), 1)
    row = lane % ROWS
    held = jnp.zeros((8, 128), jnp.int32)
    for r in range(ROWS):
        held = jnp.where(row == r, lengths_ref[r], held)
    return held + lane // ROWS


def pack(lse):
    sub = lax.broadcasted_iota(jnp.int32, (128, 128), 0)
    lane = lax.broadcasted_iota(jnp.int32, (128, 128), 1)
    at = lax.broadcasted_iota(jnp.int32, (16, 128), 0)
    tile = jnp.zeros((16, 128), F32)
    for t in range(STEPS):
        x = jnp.sum(jnp.where(lane == sub, lse[t], 0.0), axis=0, keepdims=True)
        high = x.astype(BF16).astype(F32)
        rest = x - high
        middle = rest.astype(BF16).astype(F32)
        for k, term in enumerate((high, middle, rest - middle)):
            tile = jnp.where(at == 2 * k + t, term, tile)
    return tile.astype(BF16)


def lane_of(place, e):
    sub = lax.broadcasted_iota(jnp.int32, (GROUP, 128), 0)
    lane = lax.broadcasted_iota(jnp.int32, (GROUP, 128), 1)
    return lane == sub * 8 + 2 * place + e


def pack_part(lse, place):
    at = lax.broadcasted_iota(jnp.int32, (16, 128), 0)
    tile = jnp.zeros((16, 128), F32)
    for t in range(STEPS):
        spread = jnp.zeros((GROUP, 128), F32)
        for e in range(2):
            k = e * 32 + t * 16
            spread = jnp.where(lane_of(place, e), lse[k : k + 16], spread)
        x = jnp.sum(spread, axis=0, keepdims=True)
        high = x.astype(BF16).astype(F32)
        rest = x - high
        middle = rest.astype(BF16).astype(F32)
        for k, term in enumerate((high, middle, rest - middle)):
            tile = jnp.where(at == 2 * k + t, term, tile)
    return tile.astype(BF16)


def unpack(block, place):
    o = block[0:PART].astype(F32)
    tile = block[PART:BLOCK].astype(F32)
    lse = []
    for e in range(2):
        mine = lane_of(place, e)
        for t in range(STEPS):
            x = tile[t : t + 1] + tile[2 + t : 3 + t] + tile[4 + t : 5 + t]
            spread = jnp.where(mine, jnp.broadcast_to(x, (GROUP, 128)), 0.0)
            lse.append(jnp.sum(spread, axis=1, keepdims=True))
    return o, jnp.concatenate(lse, axis=0)


def merge(state, parts):
    top = parts[0][1] if state is None else state[0]
    for _, lse in parts:
        top = jnp.maximum(top, lse)
    total, weighted = None, None
    if state is not None:
        factor = jnp.exp2(state[0] - top)
        total, weighted = state[1] * factor, state[2] * factor
    for o, lse in parts:
        factor = jnp.exp2(lse - top)
        total = factor if total is None else total + factor
        weighted = o * factor if weighted is None else weighted + o * factor
    return top, total, weighted


def order(me, plane):
    across, high = me // 2, me % 2
    units = [
        ((across + dx) % 4) * 2 + (high + dy) % 2
        for dx, dy in ((0, 0), (0, 1), (1, 0), (3, 0), (1, 1), (3, 1), (2, 0), (2, 1))
    ]

    def is_far(u):
        f = (u - plane + UNITS) % UNITS
        return (f >= 2) & (f <= 6)

    def rank(u):
        f = (u - plane + UNITS) % UNITS
        return jnp.where(f == 7, 0, jnp.where(f == 1, 1, 2))

    one = jnp.int32(1)
    count = one
    for u in units[1:]:
        count = count + jnp.where(is_far(u), 1, 0)
    own_rank = jnp.where(is_far(me), 3, rank(me))
    held_back = (plane + 2) % UNITS
    places, n = [jnp.int32(0)], one
    for u in units[1:]:
        near_place = count + rank(u) - jnp.where(own_rank < rank(u), 1, 0)
        late = (u == held_back) & jnp.logical_not(is_far(me))
        places.append(jnp.where(late, count - 1, jnp.where(is_far(u), n, near_place)))
        n = n + jnp.where(is_far(u) & jnp.logical_not(late), 1, 0)

    def unit_at(i):
        return sum(jnp.where(at == i, u, 0) for u, at in zip(units, places))

    def position(v):
        return sum(jnp.where(u == v, at, 0) for u, at in zip(units, places))

    return units, position, unit_at, is_far


def attend(
    lengths_hbm, q_hbm, kv_hbm, out_ref,
    lengths, kv, qs, hide, s0, s1, spill, psend, precv, zsend, recv,
    kv_sem, own_sem, len_sem, q_out, q_in, p_out, p_in, m_out, m_in, z_out,
):
    scores = (s0, s1)
    me = lax.axis_index("kv")
    ctx = lax.axis_index("ctx")
    plane = ctx // 4
    place = ctx % 4
    flip = 2 - 4 * (place // 2)
    units, position, unit_at, is_far = order(me, plane)

    def kv_copy(p):
        return pltpu.make_async_copy(kv_hbm.at[0, p], kv.at[p], kv_sem.at[p])

    def peer(k):
        return (k, ctx + ((k + me) % 2) * flip)

    def query_copy(k, source):
        return pltpu.make_async_remote_copy(
            src_ref=q_hbm.at[:, pl.ds(pl.multiple_of(k * WIDE, WIDE), WIDE)],
            dst_ref=qs.at[source],
            send_sem=q_out.at[k],
            recv_sem=q_in.at[source],
            device_id=peer(k),
            device_id_type=MESH,
        )

    def part_copy(i, u, d):
        return pltpu.make_async_remote_copy(
            src_ref=psend.at[i, d],
            dst_ref=recv.at[ctx],
            send_sem=p_out.at[i, d],
            recv_sem=p_in.at[ctx],
            device_id=(me, u * 4 + d),
            device_id_type=MESH,
        )

    def arrival(source):
        return pltpu.make_async_remote_copy(
            src_ref=psend.at[0, 0],
            dst_ref=recv.at[source],
            send_sem=p_out.at[0, 0],
            recv_sem=p_in.at[source],
            device_id=(me, source),
            device_id_type=MESH,
        )

    def mate_copy(i, o):
        there = (place + o) % 4
        return pltpu.make_async_remote_copy(
            src_ref=psend.at[i, there],
            dst_ref=precv.at[i, o - 1],
            send_sem=m_out.at[i, o - 1],
            recv_sem=m_in.at[i, o - 1],
            device_id=(me, plane * 4 + there),
            device_id_type=MESH,
        )

    def far_copy(i, u):
        return pltpu.make_async_remote_copy(
            src_ref=zsend.at[i],
            dst_ref=recv.at[ctx],
            send_sem=z_out.at[i],
            recv_sem=p_in.at[ctx],
            device_id=(me, u * 4 + place),
            device_id_type=MESH,
        )

    def fresh(i, u):
        return position(u + 1 - 2 * (u % 2)) > i

    measures = pltpu.make_async_copy(lengths_hbm, lengths, len_sem)
    measures.start()
    own = pltpu.make_async_copy(
        q_hbm.at[:, pl.ds(pl.multiple_of(me * WIDE, WIDE), WIDE)], qs.at[me], own_sem
    )
    own.start()

    def fetch(i, _):
        u = unit_at(i)

        @pl.when(fresh(i, u))
        def _():
            kv_copy(u // 2).start()

        return 0

    lax.fori_loop(0, UNITS, fetch, 0)

    barrier = pltpu.get_barrier_semaphore()
    for n in range(1, UNITS):
        pl.semaphore_signal(
            barrier, inc=1, device_id=peer((me + n) % UNITS), device_id_type=MESH
        )
    greeted = UNITS - 1
    for f in range(UNITS):
        for d in range(4):
            there = ((plane + f) % UNITS) * 4
            if f == 0 and d:
                there = there + (place + d) % 4
            elif f in (1, 7):
                there = there + d
            elif f and not d:
                there = there + place
            else:
                continue
            greeted += 1
            pl.semaphore_signal(barrier, inc=1, device_id=(me, there), device_id_type=MESH)
    pl.semaphore_wait(barrier, greeted)

    def send_queries(low, high):
        for u in units[low : high + 1]:
            query_copy(u, me).start()

    send_queries(1, 3)
    measures.wait()
    limits = limit_lanes(lengths) - ctx * SPAN

    def fill(i, _):
        at_row = lax.broadcasted_iota(jnp.int32, (64, 128), 0) + i * 64
        at = pl.ds(pl.multiple_of(i * 64, 64), 64)
        hide[at, :] = jnp.where(at_row < limits[0:1, :], 0.0, -HIDE).astype(BF16)
        return 0

    lax.fori_loop(0, SPAN // 64, fill, 0)
    own.wait()

    def ready(i, u):
        @pl.when(u != me)
        def _():
            query_copy(u, u).wait_recv()

        @pl.when(fresh(i, u))
        def _():
            kv_copy(u // 2).wait()

    def marked(u):
        wide = qs[u].astype(F32)
        q = jnp.concatenate(
            [
                wide[t * 8 : t * 8 + 8, h * HEAD : (h + 1) * HEAD]
                for t in range(STEPS)
                for h in range(GROUP)
            ],
            axis=0,
        ).astype(BF16)
        i = lax.broadcasted_iota(jnp.int32, (UNIT_ROWS, 128), 0)
        lane = lax.broadcasted_iota(jnp.int32, (UNIT_ROWS, 128), 1)
        target = (i // 128) * ROWS + u * 8 + i % 8
        return jnp.concatenate([q, (lane == target).astype(BF16)], axis=1)

    ones = jnp.ones((CHUNK, 128), BF16)

    def stage(i, u, n, use, make, top):
        if u is not None:
            peak = jnp.max(top, axis=1, keepdims=True) * SCALE
            total = None
        if n is not None:
            q = marked(n)
            new_top = None
        for c in range(SPAN // CHUNK):
            at = slice(c * CHUNK, (c + 1) * CHUNK)
            if n is not None:
                k = jnp.concatenate([kv[n // 2, at, 0:HEAD], hide[at, :]], axis=1)
                s = nt(q, k)
                scores[make][:, at] = s
                for b in range(CHUNK // 128):
                    x = s[:, b * 128 : (b + 1) * 128]
                    new_top = x if new_top is None else jnp.maximum(new_top, x)
            if u is not None:
                w = jnp.exp2(scores[use][:, at] * SCALE - peak).astype(BF16)
                v = jnp.concatenate([kv[u // 2, at, HEAD : 2 * HEAD], ones], axis=1)
                part = jnp.dot(w, v, preferred_element_type=F32)
                total = part if total is None else total + part
        if u is not None:
            weight = total[:, HEAD:]
            lse = jnp.log2(weight) + peak
            sums = pack((lse[:128], lse[128:]))
            spill[...] = total[:, :HEAD] / weight
            for d in range(4):
                for e in range(2):
                    rows = spill[pl.ds(2 * d + e, 32, stride=8), :]
                    psend[i, d, e * 32 : e * 32 + 32, :] = rows.astype(BF16)
                psend[i, d, PART:BLOCK, :] = sums
        return new_top if n is not None else None

    def send_near(i, u):
        for d in range(4):

            @pl.when(u * 4 + d != ctx)
            def _():
                part_copy(i, u, d).start()

    def send(i, u):
        @pl.when(is_far(u))
        def _():
            for o in range(1, 4):
                mate_copy(i, o).start()

        @pl.when(jnp.logical_not(is_far(u)))
        def _():
            send_near(i, u)

    def pass_on(i, u):
        @pl.when(is_far(u))
        def _():
            for o in range(1, 4):
                mate_copy(i, o).wait_recv()
            parts = [unpack(psend[i, place], place)]
            for o in range(1, 4):
                parts.append(unpack(precv[i, o - 1], place))
            top, total, weighted = merge(None, parts)
            zsend[i, 0:PART, :] = (weighted / total).astype(BF16)
            zsend[i, PART:BLOCK, :] = pack_part(jnp.log2(total) + top, place)
            far_copy(i, u).start()

    ready(0, me)
    top = stage(0, None, me, 1, 0, None)
    send_queries(4, 5)
    stage(0, me, None, 0, None, top)
    send(0, me)
    second = unit_at(1)
    send_queries(6, 7)
    ready(1, second)
    top = stage(1, None, second, None, 1, None)

    def pair(h, top):
        i = 2 * h + 1
        a, b, c = unit_at(i), unit_at(i + 1), unit_at(i + 2)
        ready(i + 1, b)
        top = stage(i, a, b, 1, 0, top)
        send(i, a)

        @pl.when(h > 0)
        def _():
            pass_on(i - 2, unit_at(i - 2))

        ready(i + 2, c)
        top = stage(i + 1, b, c, 0, 1, top)
        send(i + 1, b)
        pass_on(i - 1, unit_at(i - 1))
        return top

    top = lax.fori_loop(0, 3, pair, top)
    final = unit_at(UNITS - 1)
    stage(UNITS - 1, final, None, 1, None, top)
    send_near(UNITS - 1, final)
    pass_on(UNITS - 3, unit_at(UNITS - 3))

    mine = psend[position(plane), place]
    state = merge(None, [unpack(mine, place)])

    def take(state, sources):
        for source in sources:
            arrival(source).wait_recv()
        return merge(state, [unpack(recv[source], place) for source in sources])

    state = take(state, [((plane + f) % UNITS) * 4 + place for f in range(2, 7)])
    for f in (7, 1):
        state = take(state, [((plane + f) % UNITS) * 4 + d for d in range(4)])
    parts = []
    for o in range(1, 4):
        source = plane * 4 + (place + o) % 4
        arrival(source).wait_recv()
        parts.append(unpack(recv[source], place))
    _, total, weighted = merge(state, parts)
    out = weighted / total
    for t in range(STEPS):
        for h in range(GROUP):
            k = t * GROUP + h
            both = jnp.concatenate([out[k : k + 1], out[32 + k : 33 + k]], axis=0)
            out_ref[t, :, h * HEAD : (h + 1) * HEAD] = both.astype(BF16)

    for n in range(1, UNITS):
        query_copy((me + n) % UNITS, me).wait_send()

    def sent(i, _):
        u = unit_at(i)

        @pl.when(is_far(u))
        def _():
            for o in range(1, 4):
                mate_copy(i, o).wait_send()
            far_copy(i, u).wait_send()

        @pl.when(jnp.logical_not(is_far(u)))
        def _():
            for d in range(4):

                @pl.when(u * 4 + d != ctx)
                def _():
                    part_copy(i, u, d).wait_send()

        return 0

    lax.fori_loop(0, UNITS, sent, 0)


def shards(queries, kv_cache, lengths):
    out = pl.pallas_call(
        attend,
        out_shape=jax.ShapeDtypeStruct((STEPS, 2, WIDE), BF16),
        in_specs=[pl.BlockSpec(memory_space=pltpu.HBM)] * 3,
        out_specs=pl.BlockSpec(memory_space=pltpu.VMEM),
        scratch_shapes=[
            pltpu.SMEM((ROWS,), jnp.int32),
            pltpu.VMEM((PROMPTS, SPAN, 2 * HEAD), BF16),
            pltpu.VMEM((UNITS, STEPS * 8, WIDE), BF16),
            pltpu.VMEM((SPAN, 128), BF16),
            pltpu.VMEM((UNIT_ROWS, SPAN), F32),
            pltpu.VMEM((UNIT_ROWS, SPAN), F32),
            pltpu.VMEM((UNIT_ROWS, HEAD), F32),
            pltpu.VMEM((UNITS, 4, BLOCK, HEAD), BF16),
            pltpu.VMEM((UNITS, 3, BLOCK, HEAD), BF16),
            pltpu.VMEM((UNITS, BLOCK, HEAD), BF16),
            pltpu.VMEM((32, BLOCK, HEAD), BF16),
            pltpu.SemaphoreType.DMA((PROMPTS,)),
            pltpu.SemaphoreType.DMA,
            pltpu.SemaphoreType.DMA,
            pltpu.SemaphoreType.DMA((UNITS,)),
            pltpu.SemaphoreType.DMA((UNITS,)),
            pltpu.SemaphoreType.DMA((UNITS, 4)),
            pltpu.SemaphoreType.DMA((32,)),
            pltpu.SemaphoreType.DMA((UNITS, 3)),
            pltpu.SemaphoreType.DMA((UNITS, 3)),
            pltpu.SemaphoreType.DMA((UNITS,)),
        ],
        compiler_params=pltpu.CompilerParams(
            vmem_limit_bytes=60 * 2**20, collective_id=0, has_side_effects=True
        ),
        name="attend",
    )(lengths, queries.reshape(STEPS * 8, UNITS * WIDE), kv_cache)
    return out


def solution(mesh):
    in_specs = (P(None, "kv", None), P("kv", None, "ctx", None), P())
    out_specs = P(None, "ctx", "kv")
    return jax.shard_map(shards, mesh=mesh, in_specs=in_specs, out_specs=out_specs, check_vma=False)
```

```python
import jax
import jax.numpy as jnp
from jax import lax
from jax.experimental import pallas as pl
from jax.experimental.pallas import tpu as pltpu
from jax.sharding import PartitionSpec as P

F32, BF16 = jnp.float32, jnp.bfloat16
STEPS, ROWS, GROUP, HEAD = 2, 64, 16, 128
UNITS, PROMPTS, SPAN = 8, 4, 4096
WIDE = GROUP * HEAD
UNIT_ROWS = STEPS * GROUP * (ROWS // UNITS)
PART = UNIT_ROWS // 4
BLOCK = PART + 16
SCALE = 1.4426950408889634 / HEAD**0.5
HIDE = 2.0**20
CHUNK = 1024
MESH = pl.DeviceIdType.MESH


def nt(a, b):
    return lax.dot_general(a, b, (((1,), (1,)), ((), ())), preferred_element_type=F32)


def limit_lanes(lengths_ref):
    lane = lax.broadcasted_iota(jnp.int32, (8, 128), 1)
    row = lane % ROWS
    held = jnp.zeros((8, 128), jnp.int32)
    for r in range(ROWS):
        held = jnp.where(row == r, lengths_ref[r], held)
    return held + lane // ROWS


def pack(lse):
    sub = lax.broadcasted_iota(jnp.int32, (128, 128), 0)
    lane = lax.broadcasted_iota(jnp.int32, (128, 128), 1)
    at = lax.broadcasted_iota(jnp.int32, (16, 128), 0)
    tile = jnp.zeros((16, 128), F32)
    for t in range(STEPS):
        x = jnp.sum(jnp.where(lane == sub, lse[t], 0.0), axis=0, keepdims=True)
        high = x.astype(BF16).astype(F32)
        rest = x - high
        middle = rest.astype(BF16).astype(F32)
        for k, term in enumerate((high, middle, rest - middle)):
            tile = jnp.where(at == 2 * k + t, term, tile)
    return tile.astype(BF16)


def lane_of(place, e):
    sub = lax.broadcasted_iota(jnp.int32, (GROUP, 128), 0)
    lane = lax.broadcasted_iota(jnp.int32, (GROUP, 128), 1)
    return lane == sub * 8 + 2 * place + e


def pack_part(lse, place):
    at = lax.broadcasted_iota(jnp.int32, (16, 128), 0)
    tile = jnp.zeros((16, 128), F32)
    for t in range(STEPS):
        spread = jnp.zeros((GROUP, 128), F32)
        for e in range(2):
            k = e * 32 + t * 16
            spread = jnp.where(lane_of(place, e), lse[k : k + 16], spread)
        x = jnp.sum(spread, axis=0, keepdims=True)
        high = x.astype(BF16).astype(F32)
        rest = x - high
        middle = rest.astype(BF16).astype(F32)
        for k, term in enumerate((high, middle, rest - middle)):
            tile = jnp.where(at == 2 * k + t, term, tile)
    return tile.astype(BF16)


def unpack(block, place):
    o = block[0:PART].astype(F32)
    tile = block[PART:BLOCK].astype(F32)
    lse = []
    for e in range(2):
        mine = lane_of(place, e)
        for t in range(STEPS):
            x = tile[t : t + 1] + tile[2 + t : 3 + t] + tile[4 + t : 5 + t]
            spread = jnp.where(mine, jnp.broadcast_to(x, (GROUP, 128)), 0.0)
            lse.append(jnp.sum(spread, axis=1, keepdims=True))
    return o, jnp.concatenate(lse, axis=0)


def merge(state, parts):
    top = parts[0][1] if state is None else state[0]
    for _, lse in parts:
        top = jnp.maximum(top, lse)
    total, weighted = None, None
    if state is not None:
        factor = jnp.exp2(state[0] - top)
        total, weighted = state[1] * factor, state[2] * factor
    for o, lse in parts:
        factor = jnp.exp2(lse - top)
        total = factor if total is None else total + factor
        weighted = o * factor if weighted is None else weighted + o * factor
    return top, total, weighted


def order(me, plane):
    across, high = me // 2, me % 2
    units = [
        ((across + dx) % 4) * 2 + (high + dy) % 2
        for dx, dy in ((0, 0), (0, 1), (1, 0), (3, 0), (1, 1), (3, 1), (2, 0), (2, 1))
    ]

    def is_far(u):
        f = (u - plane + UNITS) % UNITS
        return (f >= 2) & (f <= 6)

    lower = jnp.minimum((plane + 1) % UNITS, (plane + 7) % UNITS)

    def rank(u):
        return jnp.where(u == plane, 2, jnp.where(u == lower, 0, 1))

    one = jnp.int32(1)
    count = one
    for u in units[1:]:
        count = count + jnp.where(is_far(u), 1, 0)
    own_rank = jnp.where(is_far(me), 3, rank(me))
    last_far = jnp.maximum((plane + 2) % UNITS, (plane + 6) % UNITS)
    other = jnp.maximum((plane + 3) % UNITS, (plane + 5) % UNITS)
    last_far = jnp.where(last_far == me, other, last_far)
    places, n = [jnp.int32(0)], one
    for u in units[1:]:
        near_place = count + rank(u) - jnp.where(own_rank < rank(u), 1, 0)
        places.append(jnp.where(u == last_far, count - 1, jnp.where(is_far(u), n, near_place)))
        n = n + jnp.where(is_far(u) & (u != last_far), 1, 0)

    def unit_at(i):
        return sum(jnp.where(at == i, u, 0) for u, at in zip(units, places))

    def position(v):
        return sum(jnp.where(u == v, at, 0) for u, at in zip(units, places))

    return units, position, unit_at, is_far


def attend(
    lengths_hbm, q_hbm, kv_hbm, out_ref,
    lengths, kv, qs, hide, s0, s1, spill, psend, precv, zsend, recv,
    kv_sem, own_sem, len_sem, q_out, q_in, b_out, b_in, m_in,
):
    scores = (s0, s1)
    me = lax.axis_index("kv")
    ctx = lax.axis_index("ctx")
    plane = ctx // 4
    place = ctx % 4
    flip = 2 - 4 * (place // 2)
    units, position, unit_at, is_far = order(me, plane)

    def kv_copy(p):
        return pltpu.make_async_copy(kv_hbm.at[0, p], kv.at[p], kv_sem.at[p])

    def peer(k):
        return (k, ctx + ((k + me) % 2) * flip)

    def query_copy(k, source):
        return pltpu.make_async_remote_copy(
            src_ref=q_hbm.at[:, pl.ds(pl.multiple_of(k * WIDE, WIDE), WIDE)],
            dst_ref=qs.at[source],
            send_sem=q_out,
            recv_sem=q_in.at[source],
            device_id=peer(k),
            device_id_type=MESH,
        )

    def part_copy(i, u, d):
        return pltpu.make_async_remote_copy(
            src_ref=psend.at[i, d],
            dst_ref=recv.at[ctx],
            send_sem=b_out,
            recv_sem=b_in.at[jnp.where(u == plane, 2, 1)],
            device_id=(me, u * 4 + d),
            device_id_type=MESH,
        )

    def blocks(ref, count, sem):
        return pltpu.make_async_remote_copy(
            src_ref=ref.at[pl.ds(0, count)],
            dst_ref=ref.at[pl.ds(0, count)],
            send_sem=sem,
            recv_sem=sem,
            device_id=(me, ctx),
            device_id_type=MESH,
        )

    def mate_copy(i, o):
        there = (place + o) % 4
        return pltpu.make_async_remote_copy(
            src_ref=psend.at[i, there],
            dst_ref=precv.at[i, o - 1],
            send_sem=b_out,
            recv_sem=m_in.at[i],
            device_id=(me, plane * 4 + there),
            device_id_type=MESH,
        )

    def far_copy(i, u):
        return pltpu.make_async_remote_copy(
            src_ref=zsend.at[i],
            dst_ref=recv.at[ctx],
            send_sem=b_out,
            recv_sem=b_in.at[0],
            device_id=(me, u * 4 + place),
            device_id_type=MESH,
        )

    def fresh(i, u):
        return position(u + 1 - 2 * (u % 2)) > i

    measures = pltpu.make_async_copy(lengths_hbm, lengths, len_sem)
    measures.start()
    own = pltpu.make_async_copy(
        q_hbm.at[:, pl.ds(pl.multiple_of(me * WIDE, WIDE), WIDE)], qs.at[me], own_sem
    )
    own.start()

    def fetch(i, _):
        u = unit_at(i)

        @pl.when(fresh(i, u))
        def _():
            kv_copy(u // 2).start()

        return 0

    lax.fori_loop(0, UNITS, fetch, 0)

    barrier = pltpu.get_barrier_semaphore()
    for n in range(1, UNITS):
        pl.semaphore_signal(
            barrier, inc=1, device_id=peer((me + n) % UNITS), device_id_type=MESH
        )
    greeted = UNITS - 1
    for f in range(UNITS):
        for d in range(4):
            there = ((plane + f) % UNITS) * 4
            if f == 0 and d:
                there = there + (place + d) % 4
            elif f in (1, 7):
                there = there + d
            elif f and not d:
                there = there + place
            else:
                continue
            greeted += 1
            pl.semaphore_signal(barrier, inc=1, device_id=(me, there), device_id_type=MESH)
    pl.semaphore_wait(barrier, greeted)

    def send_queries(low, high):
        for u in units[low : high + 1]:
            query_copy(u, me).start()

    send_queries(1, 3)
    measures.wait()
    limits = limit_lanes(lengths) - ctx * SPAN

    def fill(i, _):
        at_row = lax.broadcasted_iota(jnp.int32, (64, 128), 0) + i * 64
        at = pl.ds(pl.multiple_of(i * 64, 64), 64)
        hide[at, :] = jnp.where(at_row < limits[0:1, :], 0.0, -HIDE).astype(BF16)
        return 0

    lax.fori_loop(0, SPAN // 64, fill, 0)
    send_queries(4, 5)
    own.wait()

    def ready(i, u):
        @pl.when(u != me)
        def _():
            query_copy(u, u).wait_recv()

        @pl.when(fresh(i, u))
        def _():
            kv_copy(u // 2).wait()

    def marked(u):
        wide = qs[u].astype(F32)
        q = jnp.concatenate(
            [
                wide[t * 8 : t * 8 + 8, h * HEAD : (h + 1) * HEAD]
                for t in range(STEPS)
                for h in range(GROUP)
            ],
            axis=0,
        ).astype(BF16)
        i = lax.broadcasted_iota(jnp.int32, (UNIT_ROWS, 128), 0)
        lane = lax.broadcasted_iota(jnp.int32, (UNIT_ROWS, 128), 1)
        target = (i // 128) * ROWS + u * 8 + i % 8
        return jnp.concatenate([q, (lane == target).astype(BF16)], axis=1)

    ones = jnp.ones((CHUNK, 128), BF16)

    def stage(i, u, n, use, make, top):
        if u is not None:
            peak = jnp.max(top, axis=1, keepdims=True) * SCALE
            total = None
        if n is not None:
            q = marked(n)
            new_top = None
        for c in range(SPAN // CHUNK):
            at = slice(c * CHUNK, (c + 1) * CHUNK)
            if n is not None:
                k = jnp.concatenate([kv[n // 2, at, 0:HEAD], hide[at, :]], axis=1)
                s = nt(q, k)
                scores[make][:, at] = s
                for b in range(CHUNK // 128):
                    x = s[:, b * 128 : (b + 1) * 128]
                    new_top = x if new_top is None else jnp.maximum(new_top, x)
            if u is not None:
                w = jnp.exp2(scores[use][:, at] * SCALE - peak).astype(BF16)
                v = jnp.concatenate([kv[u // 2, at, HEAD : 2 * HEAD], ones], axis=1)
                part = jnp.dot(w, v, preferred_element_type=F32)
                total = part if total is None else total + part
        if u is not None:
            weight = total[:, HEAD:]
            lse = jnp.log2(weight) + peak
            sums = pack((lse[:128], lse[128:]))
            spill[...] = total[:, :HEAD] / weight
            for d in range(4):
                for e in range(2):
                    rows = spill[pl.ds(2 * d + e, 32, stride=8), :]
                    psend[i, d, e * 32 : e * 32 + 32, :] = rows.astype(BF16)
                psend[i, d, PART:BLOCK, :] = sums
        return new_top if n is not None else None

    def send_mates(i):
        for o in range(1, 4):
            mate_copy(i, o).start()

    def send_near(i, u):
        for o in range(1, 4):
            part_copy(i, u, (place + o) % 4).start()

        @pl.when(u != plane)
        def _():
            part_copy(i, u, place).start()

    def send(i, u):
        @pl.when(is_far(u))
        def _():
            send_mates(i)

        @pl.when(jnp.logical_not(is_far(u)))
        def _():
            send_near(i, u)

    def pass_on(i, u):
        blocks(recv, 3, m_in.at[i]).wait_recv()
        parts = [unpack(psend[i, place], place)]
        for o in range(1, 4):
            parts.append(unpack(precv[i, o - 1], place))
        top, total, weighted = merge(None, parts)
        zsend[i, 0:PART, :] = (weighted / total).astype(BF16)
        zsend[i, PART:BLOCK, :] = pack_part(jnp.log2(total) + top, place)
        far_copy(i, u).start()

    at = [unit_at(i) for i in range(UNITS)]
    ready(0, me)
    top = stage(0, None, me, 1, 0, None)
    send_queries(6, 7)
    stage(0, me, None, 0, None, top)
    send(0, me)
    ready(1, at[1])
    top = stage(1, None, at[1], None, 1, None)
    for i in range(1, UNITS - 1):
        ready(i + 1, at[i + 1])
        top = stage(i, at[i], at[i + 1], i % 2, (i + 1) % 2, top)
        if i <= 4:
            send_mates(i)
        elif i == 5:
            send(i, at[i])
        else:
            send_near(i, at[i])
        if i == 3:

            @pl.when(is_far(me))
            def _():
                pass_on(0, me)

        elif i > 3:
            pass_on(i - 3, at[i - 3])
    stage(UNITS - 1, at[UNITS - 1], None, 1, None, top)
    send_near(UNITS - 1, at[UNITS - 1])

    pass_on(4, at[4])

    @pl.when(is_far(at[5]))
    def _():
        pass_on(5, at[5])

    mine = psend[position(plane), place]
    state = merge(None, [unpack(mine, place)])

    def take(state, sources, kind):
        blocks(recv, len(sources), b_in.at[kind]).wait_recv()
        return merge(state, [unpack(recv[source], place) for source in sources])

    state = take(state, [((plane + f) % UNITS) * 4 + place for f in range(2, 7)], 0)
    state = take(state, [plane * 4 + (place + o) % 4 for o in range(1, 4)], 2)
    sources = [((plane + f) % UNITS) * 4 + d for f in (1, 7) for d in range(4)]
    _, total, weighted = take(state, sources, 1)
    out = weighted / total
    for t in range(STEPS):
        for h in range(GROUP):
            k = t * GROUP + h
            both = jnp.concatenate([out[k : k + 1], out[32 + k : 33 + k]], axis=0)
            out_ref[t, :, h * HEAD : (h + 1) * HEAD] = both.astype(BF16)

    pltpu.make_async_remote_copy(
        src_ref=qs.at[pl.ds(0, UNITS - 1)],
        dst_ref=qs.at[pl.ds(0, UNITS - 1)],
        send_sem=q_out,
        recv_sem=q_out,
        device_id=(me, ctx),
        device_id_type=MESH,
    ).wait_send()
    blocks(recv, 5 * 4 + 2 * 4 + 3, b_out).wait_send()


def shards(queries, kv_cache, lengths):
    out = pl.pallas_call(
        attend,
        out_shape=jax.ShapeDtypeStruct((STEPS, 2, WIDE), BF16),
        in_specs=[pl.BlockSpec(memory_space=pltpu.HBM)] * 3,
        out_specs=pl.BlockSpec(memory_space=pltpu.VMEM),
        scratch_shapes=[
            pltpu.SMEM((ROWS,), jnp.int32),
            pltpu.VMEM((PROMPTS, SPAN, 2 * HEAD), BF16),
            pltpu.VMEM((UNITS, STEPS * 8, WIDE), BF16),
            pltpu.VMEM((SPAN, 128), BF16),
            pltpu.VMEM((UNIT_ROWS, SPAN), F32),
            pltpu.VMEM((UNIT_ROWS, SPAN), F32),
            pltpu.VMEM((UNIT_ROWS, HEAD), F32),
            pltpu.VMEM((UNITS, 4, BLOCK, HEAD), BF16),
            pltpu.VMEM((UNITS, 3, BLOCK, HEAD), BF16),
            pltpu.VMEM((UNITS, BLOCK, HEAD), BF16),
            pltpu.VMEM((32, BLOCK, HEAD), BF16),
            pltpu.SemaphoreType.DMA((PROMPTS,)),
            pltpu.SemaphoreType.DMA,
            pltpu.SemaphoreType.DMA,
            pltpu.SemaphoreType.DMA,
            pltpu.SemaphoreType.DMA((UNITS,)),
            pltpu.SemaphoreType.DMA,
            pltpu.SemaphoreType.DMA((3,)),
            pltpu.SemaphoreType.DMA((UNITS,)),
        ],
        compiler_params=pltpu.CompilerParams(
            vmem_limit_bytes=60 * 2**20, collective_id=0, has_side_effects=True
        ),
        name="attend",
    )(lengths, queries.reshape(STEPS * 8, UNITS * WIDE), kv_cache)
    return out


def solution(mesh):
    in_specs = (P(None, "kv", None), P("kv", None, "ctx", None), P())
    out_specs = P(None, "ctx", "kv")
    return jax.shard_map(shards, mesh=mesh, in_specs=in_specs, out_specs=out_specs, check_vma=False)
```

```python
import jax
import jax.numpy as jnp
from jax import lax
from jax.experimental import pallas as pl
from jax.experimental.pallas import tpu as pltpu
from jax.sharding import PartitionSpec as P

F32, BF16 = jnp.float32, jnp.bfloat16
STEPS, ROWS, GROUP, HEAD = 2, 64, 16, 128
UNITS, PROMPTS, SPAN = 8, 4, 4096
WIDE = GROUP * HEAD
UNIT_ROWS = STEPS * GROUP * (ROWS // UNITS)
PART = UNIT_ROWS // 4
BLOCK = PART + 16
SCALE = 1.4426950408889634 / HEAD**0.5
HIDE = 2.0**20
CHUNK = 512
MESH = pl.DeviceIdType.MESH


def nt(a, b):
    return lax.dot_general(a, b, (((1,), (1,)), ((), ())), preferred_element_type=F32)


def limit_lanes(lengths_ref):
    lane = lax.broadcasted_iota(jnp.int32, (8, 128), 1)
    row = lane % ROWS
    held = jnp.zeros((8, 128), jnp.int32)
    for r in range(ROWS):
        held = jnp.where(row == r, lengths_ref[r], held)
    return held + lane // ROWS


def pack(lse):
    sub = lax.broadcasted_iota(jnp.int32, (128, 128), 0)
    lane = lax.broadcasted_iota(jnp.int32, (128, 128), 1)
    at = lax.broadcasted_iota(jnp.int32, (16, 128), 0)
    tile = jnp.zeros((16, 128), F32)
    for t in range(STEPS):
        x = jnp.sum(jnp.where(lane == sub, lse[t], 0.0), axis=0, keepdims=True)
        high = x.astype(BF16).astype(F32)
        rest = x - high
        middle = rest.astype(BF16).astype(F32)
        for k, term in enumerate((high, middle, rest - middle)):
            tile = jnp.where(at == 2 * k + t, term, tile)
    return tile.astype(BF16)


def lane_of(place, e):
    sub = lax.broadcasted_iota(jnp.int32, (GROUP, 128), 0)
    lane = lax.broadcasted_iota(jnp.int32, (GROUP, 128), 1)
    return lane == sub * 8 + 2 * place + e


def pack_part(lse, place):
    at = lax.broadcasted_iota(jnp.int32, (16, 128), 0)
    tile = jnp.zeros((16, 128), F32)
    for t in range(STEPS):
        spread = jnp.zeros((GROUP, 128), F32)
        for e in range(2):
            k = e * 32 + t * 16
            spread = jnp.where(lane_of(place, e), lse[k : k + 16], spread)
        x = jnp.sum(spread, axis=0, keepdims=True)
        high = x.astype(BF16).astype(F32)
        rest = x - high
        middle = rest.astype(BF16).astype(F32)
        for k, term in enumerate((high, middle, rest - middle)):
            tile = jnp.where(at == 2 * k + t, term, tile)
    return tile.astype(BF16)


def unpack(block, place):
    o = block[0:PART].astype(F32)
    tile = block[PART:BLOCK].astype(F32)
    lse = []
    for e in range(2):
        mine = lane_of(place, e)
        for t in range(STEPS):
            x = tile[t : t + 1] + tile[2 + t : 3 + t] + tile[4 + t : 5 + t]
            spread = jnp.where(mine, jnp.broadcast_to(x, (GROUP, 128)), 0.0)
            lse.append(jnp.sum(spread, axis=1, keepdims=True))
    return o, jnp.concatenate(lse, axis=0)


def merge(state, parts):
    top = parts[0][1] if state is None else state[0]
    for _, lse in parts:
        top = jnp.maximum(top, lse)
    total, weighted = None, None
    if state is not None:
        factor = jnp.exp2(state[0] - top)
        total, weighted = state[1] * factor, state[2] * factor
    for o, lse in parts:
        factor = jnp.exp2(lse - top)
        total = factor if total is None else total + factor
        weighted = o * factor if weighted is None else weighted + o * factor
    return top, total, weighted


def order(me, plane):
    across, high = me // 2, me % 2
    units = [
        ((across + dx) % 4) * 2 + (high + dy) % 2
        for dx, dy in ((0, 0), (0, 1), (1, 0), (3, 0), (1, 1), (3, 1), (2, 0), (2, 1))
    ]

    def is_far(u):
        f = (u - plane + UNITS) % UNITS
        return (f >= 2) & (f <= 6)

    lower = jnp.minimum((plane + 1) % UNITS, (plane + 7) % UNITS)

    def rank(u):
        early = jnp.where(plane < 4, 1, 0)
        return jnp.where(u == plane, 2 - early, jnp.where(u == lower, 0, 1 + early))

    one = jnp.int32(1)
    count = one
    for u in units[1:]:
        count = count + jnp.where(is_far(u), 1, 0)
    own_rank = jnp.where(is_far(me), 3, rank(me))
    last_far = jnp.maximum((plane + 2) % UNITS, (plane + 6) % UNITS)
    other = jnp.maximum((plane + 3) % UNITS, (plane + 5) % UNITS)
    last_far = jnp.where(last_far == me, other, last_far)
    places, n = [jnp.int32(0)], one
    for u in units[1:]:
        near_place = count + rank(u) - jnp.where(own_rank < rank(u), 1, 0)
        places.append(jnp.where(u == last_far, count - 1, jnp.where(is_far(u), n, near_place)))
        n = n + jnp.where(is_far(u) & (u != last_far), 1, 0)

    def unit_at(i):
        return sum(jnp.where(at == i, u, 0) for u, at in zip(units, places))

    def position(v):
        return sum(jnp.where(u == v, at, 0) for u, at in zip(units, places))

    return units, position, unit_at, is_far


def attend(
    lengths_hbm, q_hbm, kv_hbm, out_ref,
    lengths, kv, qs, hide, s0, s1, spill, psend, precv, zsend, recv,
    kv_sem, own_sem, len_sem, q_out, q_in, b_out, b_in, m_in,
):
    scores = (s0, s1)
    me = lax.axis_index("kv")
    ctx = lax.axis_index("ctx")
    plane = ctx // 4
    place = ctx % 4
    flip = 2 - 4 * (place // 2)

    def kv_copy(p):
        return pltpu.make_async_copy(kv_hbm.at[0, p], kv.at[p], kv_sem.at[p])

    def peer(k):
        return (k, ctx + ((k + me) % 2) * flip)

    def query_copy(k, source):
        return pltpu.make_async_remote_copy(
            src_ref=q_hbm.at[:, pl.ds(pl.multiple_of(k * WIDE, WIDE), WIDE)],
            dst_ref=qs.at[source],
            send_sem=q_out,
            recv_sem=q_in.at[source],
            device_id=peer(k),
            device_id_type=MESH,
        )

    def part_copy(i, u, d):
        return pltpu.make_async_remote_copy(
            src_ref=psend.at[i, d],
            dst_ref=recv.at[ctx],
            send_sem=b_out,
            recv_sem=b_in.at[jnp.where(u == plane, 2, jnp.where(u == (plane + 1) % UNITS, 3, 1))],
            device_id=(me, u * 4 + d),
            device_id_type=MESH,
        )

    def blocks(ref, count, sem):
        return pltpu.make_async_remote_copy(
            src_ref=ref.at[pl.ds(0, count)],
            dst_ref=ref.at[pl.ds(0, count)],
            send_sem=sem,
            recv_sem=sem,
            device_id=(me, ctx),
            device_id_type=MESH,
        )

    def mate_copy(i, o):
        there = (place + o) % 4
        return pltpu.make_async_remote_copy(
            src_ref=psend.at[i, there],
            dst_ref=precv.at[i, o - 1],
            send_sem=b_out,
            recv_sem=m_in.at[i],
            device_id=(me, plane * 4 + there),
            device_id_type=MESH,
        )

    def far_copy(i, u):
        return pltpu.make_async_remote_copy(
            src_ref=zsend.at[i],
            dst_ref=recv.at[ctx],
            send_sem=b_out,
            recv_sem=b_in.at[0],
            device_id=(me, u * 4 + place),
            device_id_type=MESH,
        )

    kv_copy(me // 2).start()
    barrier = pltpu.get_barrier_semaphore()
    for n in range(1, UNITS):
        pl.semaphore_signal(
            barrier, inc=1, device_id=peer((me + n) % UNITS), device_id_type=MESH
        )
    greeted = UNITS - 1
    for f in range(UNITS):
        for d in range(4):
            there = ((plane + f) % UNITS) * 4
            if f == 0 and d:
                there = there + (place + d) % 4
            elif f in (1, 7):
                there = there + d
            elif f and not d:
                there = there + place
            else:
                continue
            greeted += 1
            pl.semaphore_signal(barrier, inc=1, device_id=(me, there), device_id_type=MESH)
    units, position, unit_at, is_far = order(me, plane)
    measures = pltpu.make_async_copy(lengths_hbm, lengths, len_sem)
    measures.start()
    own = pltpu.make_async_copy(
        q_hbm.at[:, pl.ds(pl.multiple_of(me * WIDE, WIDE), WIDE)], qs.at[me], own_sem
    )
    own.start()
    others = [(me // 2 + n) % PROMPTS for n in range(1, PROMPTS)]
    for p in others:
        kv_copy(p).start()
    pl.semaphore_wait(barrier, greeted)

    def send_queries(low, high):
        for u in units[low : high + 1]:
            query_copy(u, me).start()

    send_queries(1, 3)
    measures.wait()
    limits = limit_lanes(lengths) - ctx * SPAN

    def fill(i, _):
        at_row = lax.broadcasted_iota(jnp.int32, (64, 128), 0) + i * 64
        at = pl.ds(pl.multiple_of(i * 64, 64), 64)
        hide[at, :] = jnp.where(at_row < limits[0:1, :], 0.0, -HIDE).astype(BF16)
        return 0

    lax.fori_loop(0, SPAN // 64, fill, 0)
    send_queries(4, 5)
    own.wait()

    def marked(u):
        wide = qs[u].astype(F32)
        q = jnp.concatenate(
            [
                wide[t * 8 : t * 8 + 8, h * HEAD : (h + 1) * HEAD]
                for t in range(STEPS)
                for h in range(GROUP)
            ],
            axis=0,
        ).astype(BF16)
        i = lax.broadcasted_iota(jnp.int32, (UNIT_ROWS, 128), 0)
        lane = lax.broadcasted_iota(jnp.int32, (UNIT_ROWS, 128), 1)
        target = (i // 128) * ROWS + u * 8 + i % 8
        return jnp.concatenate([q, (lane == target).astype(BF16)], axis=1)

    ones = jnp.ones((CHUNK, 128), BF16)

    def stage(i, u, n, use, make, top):
        if u is not None:
            peak = jnp.max(top, axis=1, keepdims=True) * SCALE
            total = None
        if n is not None:
            q = marked(n)
            new_top = None
        for c in range(SPAN // CHUNK):
            at = slice(c * CHUNK, (c + 1) * CHUNK)
            if n is not None:
                k = jnp.concatenate([kv[n // 2, at, 0:HEAD], hide[at, :]], axis=1)
                s = nt(q, k)
                scores[make][:, at] = s
                for b in range(CHUNK // 128):
                    x = s[:, b * 128 : (b + 1) * 128]
                    new_top = x if new_top is None else jnp.maximum(new_top, x)
            if u is not None:
                w = jnp.exp2(scores[use][:, at] * SCALE - peak).astype(BF16)
                v = jnp.concatenate([kv[u // 2, at, HEAD : 2 * HEAD], ones], axis=1)
                part = jnp.dot(w, v, preferred_element_type=F32)
                total = part if total is None else total + part
        if u is not None:
            weight = total[:, HEAD:]
            lse = jnp.log2(weight) + peak
            sums = pack((lse[:128], lse[128:]))
            spill[...] = total[:, :HEAD] / weight
            for d in range(4):
                for e in range(2):
                    rows = spill[pl.ds(2 * d + e, 32, stride=8), :]
                    psend[i, d, e * 32 : e * 32 + 32, :] = rows.astype(BF16)
                psend[i, d, PART:BLOCK, :] = sums
        return new_top if n is not None else None

    def send_mates(i):
        for o in range(1, 4):
            mate_copy(i, o).start()

    def send_near(i, u):
        for o in range(1, 4):
            part_copy(i, u, (place + o) % 4).start()

        @pl.when(u != plane)
        def _():
            part_copy(i, u, place).start()

    def send(i, u):
        @pl.when(is_far(u))
        def _():
            send_mates(i)

        @pl.when(jnp.logical_not(is_far(u)))
        def _():
            send_near(i, u)

    def pass_on(i, u):
        blocks(recv, 3, m_in.at[i]).wait_recv()
        parts = [unpack(psend[i, place], place)]
        for o in range(1, 4):
            parts.append(unpack(precv[i, o - 1], place))
        top, total, weighted = merge(None, parts)
        zsend[i, 0:PART, :] = (weighted / total).astype(BF16)
        zsend[i, PART:BLOCK, :] = pack_part(jnp.log2(total) + top, place)
        far_copy(i, u).start()

    at = [unit_at(i) for i in range(UNITS)]
    kv_copy(me // 2).wait()
    top = stage(0, None, me, 1, 0, None)
    send_queries(6, 7)
    stage(0, me, None, 0, None, top)
    send(0, me)
    for p in others:
        kv_copy(p).wait()
    query_copy(at[1], at[1]).wait_recv()
    top = stage(1, None, at[1], None, 1, None)
    for i in range(1, UNITS - 1):
        query_copy(at[i + 1], at[i + 1]).wait_recv()
        top = stage(i, at[i], at[i + 1], i % 2, (i + 1) % 2, top)
        if i <= 4:
            send_mates(i)
        elif i == 5:
            send(i, at[i])
        else:
            send_near(i, at[i])
        if i == 3:

            @pl.when(is_far(me))
            def _():
                pass_on(0, me)

        elif i > 3:
            pass_on(i - 3, at[i - 3])
    stage(UNITS - 1, at[UNITS - 1], None, 1, None, top)
    send_near(UNITS - 1, at[UNITS - 1])

    pass_on(4, at[4])

    @pl.when(is_far(at[5]))
    def _():
        pass_on(5, at[5])

    mine = psend[position(plane), place]
    state = merge(None, [unpack(mine, place)])

    def take(state, sources, kind):
        blocks(recv, len(sources), b_in.at[kind]).wait_recv()
        return merge(state, [unpack(recv[source], place) for source in sources])

    state = take(state, [((plane + f) % UNITS) * 4 + place for f in range(2, 7)], 0)
    state = take(state, [plane * 4 + (place + o) % 4 for o in range(1, 4)], 2)
    state = take(state, [((plane + 1) % UNITS) * 4 + d for d in range(4)], 1)
    _, total, weighted = take(state, [((plane + 7) % UNITS) * 4 + d for d in range(4)], 3)
    out = weighted / total
    for t in range(STEPS):
        for h in range(GROUP):
            k = t * GROUP + h
            both = jnp.concatenate([out[k : k + 1], out[32 + k : 33 + k]], axis=0)
            out_ref[t, :, h * HEAD : (h + 1) * HEAD] = both.astype(BF16)

    pltpu.make_async_remote_copy(
        src_ref=qs.at[pl.ds(0, UNITS - 1)],
        dst_ref=qs.at[pl.ds(0, UNITS - 1)],
        send_sem=q_out,
        recv_sem=q_out,
        device_id=(me, ctx),
        device_id_type=MESH,
    ).wait_send()
    blocks(recv, 5 * 4 + 2 * 4 + 3, b_out).wait_send()


def shards(queries, kv_cache, lengths):
    out = pl.pallas_call(
        attend,
        out_shape=jax.ShapeDtypeStruct((STEPS, 2, WIDE), BF16),
        in_specs=[pl.BlockSpec(memory_space=pltpu.HBM)] * 3,
        out_specs=pl.BlockSpec(memory_space=pltpu.VMEM),
        scratch_shapes=[
            pltpu.SMEM((ROWS,), jnp.int32),
            pltpu.VMEM((PROMPTS, SPAN, 2 * HEAD), BF16),
            pltpu.VMEM((UNITS, STEPS * 8, WIDE), BF16),
            pltpu.VMEM((SPAN, 128), BF16),
            pltpu.VMEM((UNIT_ROWS, SPAN), F32),
            pltpu.VMEM((UNIT_ROWS, SPAN), F32),
            pltpu.VMEM((UNIT_ROWS, HEAD), F32),
            pltpu.VMEM((UNITS, 4, BLOCK, HEAD), BF16),
            pltpu.VMEM((UNITS, 3, BLOCK, HEAD), BF16),
            pltpu.VMEM((UNITS, BLOCK, HEAD), BF16),
            pltpu.VMEM((32, BLOCK, HEAD), BF16),
            pltpu.SemaphoreType.DMA((PROMPTS,)),
            pltpu.SemaphoreType.DMA,
            pltpu.SemaphoreType.DMA,
            pltpu.SemaphoreType.DMA,
            pltpu.SemaphoreType.DMA((UNITS,)),
            pltpu.SemaphoreType.DMA,
            pltpu.SemaphoreType.DMA((4,)),
            pltpu.SemaphoreType.DMA((UNITS,)),
        ],
        compiler_params=pltpu.CompilerParams(
            vmem_limit_bytes=60 * 2**20, collective_id=0, has_side_effects=True
        ),
        name="attend",
    )(lengths, queries.reshape(STEPS * 8, UNITS * WIDE), kv_cache)
    return out


def solution(mesh):
    in_specs = (P(None, "kv", None), P("kv", None, "ctx", None), P())
    out_specs = P(None, "ctx", "kv")
    return jax.shard_map(shards, mesh=mesh, in_specs=in_specs, out_specs=out_specs, check_vma=False)
```
